32 devices in a mesh: chan: 8 (over z, y), grp: 4 (over x, core).
Axes of the slice: x: 2, y: 2, z: 4, core: 2. Of those that a mesh axis runs over, the one named last changes fastest.
Arguments:
- voltages: bfloat16 [512, 2, 139, 1024], P(('chan', 'grp')), may hold values from -6 to 6
- filter_taps: float32 [12, 512], replicated, may hold values from -1.75 to 1.75
- chan_index: int32 [96], replicated, may hold values from 0 to 511
- beam_weights: bfloat16 [96, 4096, 2, 512], P('chan', 'grp'), may hold values from -0.1875 to 0.1875
Outputs:
- beams: bfloat16 [96, 4096, 2, 2, 128], P('chan', 'grp')
The draws below stay inside these ranges and needn't reach their ends.
Inputs may be any that keep to these rules, and one draw needn't show every extreme that they name: `chan_index`: filterbank channel numbers; a channel may be selected more than once.
All inputs are finite; a program needn't handle non-finite values.
Results may differ from the reference program's by a relative error of at most 0.0065.
Values may be sent and summed in bfloat16 or wider, within the bound.
No kernel may reach another device: no remote copies, remote signals or barrier semaphores. Data moves between devices by JAX's collectives and lax.ppermute only.
A program may use at most 192 MiB of HBM per device.

```python
import math
import jax
import jax.numpy as jnp
from jax import lax

STATIONS = 512
POLS = 2
NFFT = 512
TAPS = 12
BEAMS = 4096
NSEL = 96
BLOCKS = 139


def place_ends(values, stream_key, least, high):
    longest = values.shape.index(max(values.shape))
    spots = []
    for shift in (0, 1):
        where = [jax.random.randint(jax.random.fold_in(stream_key, axis), (), 0, length) for axis, length in enumerate(values.shape)]
        where[longest] = (where[longest] + shift) % values.shape[longest]
        spots.append(tuple(where))
    return values.at[spots[0]].set(least).at[spots[1]].set(high)


def block_levels(rng, extent, pieces, smallest, largest):
    gain = 1.0
    for dim, blocks in pieces:
        draws = jax.random.uniform(jax.random.fold_in(jax.random.fold_in(rng, 6), dim), (blocks,), jnp.float32, smallest / len(pieces), largest / len(pieces))
        gain = gain * jnp.repeat(jnp.exp(draws), extent[dim] // blocks).reshape((-1,) + (1,) * (len(extent) - 1 - dim))
    return gain


def noise(rng, shape, deviation, limit, shards=(), kind=jnp.bfloat16):
    entries = deviation * jax.random.normal(rng, shape, jnp.float32)
    if shards:
        entries = entries * block_levels(rng, shape, shards, -0.22, 0.18)
    return jnp.clip(entries, -limit, limit).astype(kind)


def setup_inputs(seed: int = 0) -> dict:
    keys = jax.random.split(jax.random.key(seed), 5)
    voltages = noise(keys[0], (STATIONS, POLS, BLOCKS, 2 * NFFT), 1.0, 6.0, ((0, 32),))
    filter_taps = noise(keys[1], (TAPS, NFFT), TAPS ** -0.5, 1.75, (), jnp.float32)
    chan_index = place_ends(jax.random.randint(keys[2], (NSEL,), 0, NFFT), jax.random.fold_in(keys[2], 1), 0, NFFT - 1).astype(jnp.int32)
    beam_weights = noise(keys[3], (NSEL, BEAMS, 2, STATIONS), (2 * STATIONS) ** -0.5, 0.1875, ((0, 8), (1, 4)))
    return dict(voltages=voltages, filter_taps=filter_taps, chan_index=chan_index, beam_weights=beam_weights)


def build_table(chan_index, fft_size):
    position = jnp.arange(fft_size, dtype=jnp.int32)
    phase = position[:, None] * chan_index[None, :].astype(jnp.int32) % fft_size
    angle = 2.0 * math.pi / fft_size * phase.astype(jnp.float32)
    factor = 1.0 / math.sqrt(fft_size)
    cosine = jnp.cos(angle) * factor
    sine = jnp.sin(angle) * factor
    upper = jnp.concatenate([cosine, -sine], axis=1)
    lower = jnp.concatenate([sine, cosine], axis=1)
    return jnp.concatenate([upper, lower], axis=0).astype(jnp.bfloat16)

def channelize(voltages, filter_taps, phase_table):
    tap_count = filter_taps.shape[0]
    spectra_count = voltages.shape[2] - tap_count + 1
    doubled = jnp.concatenate([filter_taps, filter_taps], axis=1)
    filtered = jnp.zeros(voltages.shape[:2] + (spectra_count, voltages.shape[3]), jnp.float32)
    for tap_delay in range(tap_count):
        window = voltages[:, :, tap_delay:tap_delay + spectra_count, :].astype(jnp.float32)
        filtered = filtered + window * doubled[tap_delay]
    filtered = filtered.astype(jnp.bfloat16)
    flat = filtered.reshape(-1, filtered.shape[3])
    result = jnp.dot(flat, phase_table, preferred_element_type=jnp.float32).astype(jnp.bfloat16)
    return result.reshape(voltages.shape[:2] + (spectra_count, 2, phase_table.shape[1] // 2))

def reference(voltages, filter_taps, chan_index, beam_weights):
    phase_table = build_table(chan_index, NFFT)
    grouped = voltages.reshape((STATIONS // 16, 16) + voltages.shape[1:])
    spectra = lax.map(lambda station_block: channelize(station_block, filter_taps, phase_table), grouped)
    spectra = spectra.reshape((STATIONS,) + spectra.shape[2:])
    by_channel = jnp.moveaxis(spectra, 4, 0)

    def one_channel(pair):
        weight_block, channel_data = pair
        summed = jnp.einsum('bws,spmr->bwprm', weight_block.astype(jnp.float32), channel_data.astype(jnp.float32), precision=lax.Precision.HIGHEST)
        real_part = summed[:, 0, :, 0] - summed[:, 1, :, 1]
        imag_part = summed[:, 0, :, 1] + summed[:, 1, :, 0]
        return jnp.stack([real_part, imag_part], axis=2).astype(jnp.bfloat16)
    return lax.map(one_channel, (beam_weights, by_channel))
```

```python
import math, functools
import jax, jax.numpy as jnp
from jax import lax
from jax.experimental import pallas as pl
from jax.experimental.pallas import tpu as pltpu
from jax.sharding import PartitionSpec as P

def build_table_t(chan_index, fft_size):
    position = jnp.arange(fft_size, dtype=jnp.int32)
    phase = chan_index[:, None] * position[None, :] % fft_size
    angle = 2.0 * math.pi / fft_size * phase.astype(jnp.float32)
    factor = 1.0 / math.sqrt(fft_size)
    cosine = jnp.cos(angle) * factor
    sine = jnp.sin(angle) * factor
    first = jnp.concatenate([cosine, sine], axis=1)
    second = jnp.concatenate([-sine, cosine], axis=1)
    return jnp.concatenate([first, second], axis=0).astype(jnp.bfloat16)

def chan_kernel(stations, pols, spec, taps, group, v_ref, t_ref, f_ref, o_ref, fir, acc):
    s = pl.program_id(0)
    tiles = f_ref.shape[1] // 128
    lines = tiles * pols
    half = lines // 2
    nsel = f_ref.shape[0] // 2
    tap = [t_ref[pl.ds(t * half, half), :] for t in range(taps)]

    def step(i, _):
        m0 = i * group
        x = v_ref[0, pl.ds(pl.multiple_of(m0 * lines, lines), (group + taps - 1) * lines), :]
        x = x.astype(jnp.float32).reshape(group + taps - 1, 2, half, 128)
        for h in range(2):
            for g in range(group):
                total = x[g, h] * tap[0]
                for t in range(1, taps):
                    total = total + x[g + t, h] * tap[t]
                fir[pl.ds(pl.multiple_of((m0 + g) * lines, lines) + h * half, half), :] = total
        return 0

    lax.fori_loop(0, spec // group, step, 0)
    rows = []
    for p in range(pols):
        cols = [fir[pl.ds(nt * pols + p, spec, stride=lines), :].astype(jnp.bfloat16) for nt in range(tiles)]
        rows.append(jnp.concatenate(cols, axis=1))
    filtered = jnp.concatenate(rows, axis=0)
    out = lax.dot_general(f_ref[...], filtered, (((1,), (1,)), ((), ())), preferred_element_type=jnp.float32)
    for p in range(pols):
        for r in range(2):
            acc[pl.ds((p * 2 + r) * stations + s, nsel, stride=pols * 2 * stations), :] = (
                out[r * nsel:(r + 1) * nsel, p * spec:(p + 1) * spec])

    @pl.when(s == stations - 1)
    def _():
        o_ref[...] = acc[...].astype(jnp.bfloat16)

def channelize(voltages, filter_taps, table_t, group=8):
    stations, pols, blocks, width = voltages.shape
    taps, nfft = filter_taps.shape
    spec = blocks - taps + 1
    tiles = width // 128
    nsel = table_t.shape[0] // 2
    v = voltages.transpose(0, 2, 1, 3).reshape(stations, blocks, pols, tiles, 128)
    v = v.transpose(0, 1, 3, 2, 4).reshape(stations, blocks * tiles * pols, 128)
    half = tiles // 2 * pols
    t = jnp.repeat(filter_taps.reshape(taps * nfft // 128, 128), pols, axis=0)
    rows = nsel * pols * 2 * stations
    return pl.pallas_call(
        functools.partial(chan_kernel, stations, pols, spec, taps, group),
        grid=(stations,),
        out_shape=jax.ShapeDtypeStruct((rows, 128), jnp.bfloat16),
        in_specs=[
            pl.BlockSpec((1, blocks * tiles * pols, 128), lambda s: (s, 0, 0)),
            pl.BlockSpec((taps * half, 128), lambda s: (0, 0)),
            pl.BlockSpec(table_t.shape, lambda s: (0, 0)),
        ],
        out_specs=pl.BlockSpec((rows, 128), lambda s: (0, 0)),
        scratch_shapes=[pltpu.VMEM((spec * tiles * pols, 128), jnp.float32), pltpu.VMEM((rows, 128), jnp.float32)],
        compiler_params=pltpu.CompilerParams(vmem_limit_bytes=40 << 20),
        cost_estimate=pl.CostEstimate(flops=2 * stations * pols * spec * width * (taps*16 + 2 * nsel), bytes_accessed=voltages.size * 2, transcendentals=0),
        name="channelize",
    )(v, t, table_t)

def beam_kernel(sub, pr, w_ref, x_ref, o_ref, wide, rhs, outw):
    groups, chans, _, local, m = x_ref.shape
    local = local // pr
    stations = groups * chans * local
    st_n = stations // 128
    lines = st_n * 2
    for p in range(pr // 2):
        for c in range(chans):
            for g in range(groups):
                low = (c * groups + g) * local
                re = x_ref[g, c, 0, 2 * p * local:(2 * p + 1) * local, :]
                im = x_ref[g, c, 0, (2 * p + 1) * local:(2 * p + 2) * local, :]
                rhs[low:low + local, (2 * p) * m:(2 * p + 1) * m] = re
                rhs[low:low + local, (2 * p + 1) * m:(2 * p + 2) * m] = im
                rhs[stations + low:stations + low + local, (2 * p) * m:(2 * p + 1) * m] = -im
                rhs[stations + low:stations + low + local, (2 * p + 1) * m:(2 * p + 2) * m] = re
    beams = w_ref.shape[1] // lines
    tile = beams // sub
    right = rhs[...]
    for i in range(sub):
        wide[i] = w_ref[0, i * tile * lines:(i + 1) * tile * lines, :].astype(jnp.float32)
        left = jnp.concatenate(
            [wide[i, pl.ds(st * 2 + w, tile, stride=lines), :].astype(jnp.bfloat16) for w in range(2) for st in range(st_n)], axis=1)
        out = jnp.dot(left, right, preferred_element_type=jnp.float32)
        for q in range(pr):
            outw[i, pl.ds(q, tile, stride=pr), :] = out[:, q * m:(q + 1) * m]
        o_ref[0, i * tile * pr:(i + 1) * tile * pr, :] = outw[i].astype(jnp.bfloat16)

def beams_of(weights, x, pr, sub=4):
    chans, beams, parts, stations = weights.shape
    m = x.shape[4]
    st_n = stations // 128
    w = weights.reshape(chans, beams, 2, st_n, 128).transpose(0, 1, 3, 2, 4).reshape(chans, beams * st_n * 2, 128)
    tile = beams // sub
    out = pl.pallas_call(
        functools.partial(beam_kernel, sub, pr),
        grid=(chans,),
        out_shape=jax.ShapeDtypeStruct((chans, beams * pr, 128), jnp.bfloat16),
        in_specs=[
            pl.BlockSpec((1, beams * st_n * 2, 128), lambda j: (j, 0, 0)),
            pl.BlockSpec((x.shape[0], x.shape[1], 1, x.shape[3], m), lambda j: (0, 0, j, 0, 0)),
        ],
        out_specs=pl.BlockSpec((1, beams * pr, 128), lambda j: (j, 0, 0)),
        scratch_shapes=[pltpu.VMEM((sub, tile * st_n * 2, 128), jnp.float32), pltpu.VMEM((2 * stations, pr * m), jnp.bfloat16), pltpu.VMEM((sub, tile * pr, 128), jnp.float32)],
        compiler_params=pltpu.CompilerParams(vmem_limit_bytes=48 << 20),
        name="beams",
    )(w, x)
    return out.reshape(chans, beams, pr // 2, 2, m)


def shards(voltages, filter_taps, chan_index, beam_weights):
    stations, pols = voltages.shape[:2]
    chans = lax.axis_size("chan")
    table_t = build_table_t(chan_index, filter_taps.shape[1])
    spectra = channelize(voltages, filter_taps, table_t)
    mine = beam_weights.shape[0]
    spectra = spectra.reshape(chans, mine * pols * 2 * stations, 128)
    turned = lax.all_to_all(spectra, "chan", split_axis=0, concat_axis=0, tiled=True)
    gathered = lax.all_gather(turned, "grp", axis=0, tiled=False)
    x = gathered.reshape(gathered.shape[0], chans, mine, pols, 2, stations, 128)
    if stations % 16:
        x = x.transpose(2, 3, 4, 1, 0, 5, 6)
        x = x.reshape(1, 1, mine, -1, 128)
    else:
        x = x.reshape(x.shape[0], chans, mine, pols * 2 * stations, 128)
    return beams_of(beam_weights, x, pols * 2)


def solution(mesh):
    placed = (P(("chan", "grp"), None, None, None), P(), P(), P("chan", "grp", None, None))
    return jax.shard_map(
        shards,
        mesh=mesh,
        in_specs=placed,
        out_specs=P("chan", "grp", None, None, None),
        check_vma=False,
    )
```

```python
import functools
import math

import jax
import jax.numpy as jnp
from jax import lax
from jax.experimental import pallas as pl
from jax.experimental.pallas import tpu as pltpu
from jax.sharding import PartitionSpec as P

LANES = 128


def build_table(chan_index, fft_size):
    position = jnp.arange(fft_size, dtype=jnp.int32)
    phase = chan_index[:, None] * position[None, :] % fft_size
    angle = 2.0 * math.pi / fft_size * phase.astype(jnp.float32)
    factor = 1.0 / math.sqrt(fft_size)
    cosine = jnp.cos(angle) * factor
    sine = jnp.sin(angle) * factor
    first = jnp.concatenate([cosine, sine], axis=1)
    second = jnp.concatenate([-sine, cosine], axis=1)
    return jnp.concatenate([first, second], axis=0).astype(jnp.bfloat16)


def channelize_kernel(dims, v_ref, t_ref, f_ref, *rest):
    stations, pols, spec, taps, group, chans, counts = dims
    outs, (fir, acc) = rest[: len(counts)], rest[len(counts) :]
    s = pl.program_id(0)
    tiles = v_ref.shape[1] // (spec + taps - 1) // pols
    lines = tiles * pols
    half = lines // 2
    nsel = f_ref.shape[0] // 2
    tap = [t_ref[pl.ds(t * half, half), :] for t in range(taps)]

    def step(i, _):
        m0 = i * group
        start = pl.multiple_of(m0 * lines, lines)
        x = v_ref[0, pl.ds(start, (group + taps - 1) * lines), :]
        x = x.astype(jnp.float32).reshape(group + taps - 1, 2, half, LANES)
        for h in range(2):
            for g in range(group):
                total = x[g, h] * tap[0]
                for t in range(1, taps):
                    total = total + x[g + t, h] * tap[t]
                row = pl.multiple_of((m0 + g) * lines, lines)
                fir[pl.ds(row + h * half, half), :] = total
        return 0

    lax.fori_loop(0, spec // group, step, 0)
    rows = []
    for p in range(pols):
        cols = [fir[pl.ds(n * pols + p, spec, stride=lines), :].astype(jnp.bfloat16) for n in range(tiles)]
        rows.append(jnp.concatenate(cols, axis=1))
    filtered = jnp.concatenate(rows, axis=0)
    out = lax.dot_general(f_ref[...], filtered, (((1,), (1,)), ((), ())), preferred_element_type=jnp.float32)
    for p in range(pols):
        for r in range(2):
            acc[pl.ds((p * 2 + r) * stations + s, nsel, stride=pols * 2 * stations), :] = out[
                r * nsel : (r + 1) * nsel, p * spec : (p + 1) * spec
            ]

    @pl.when(s == stations - 1)
    def _():
        size = pols * 2 * stations
        mine = nsel // chans
        for c in range(chans):
            low = c * mine * size
            for out_ref, count in zip(outs, counts):
                out_ref[c] = acc[low : low + count * size, :].astype(jnp.bfloat16)
                low += count * size


def channelize(v, taps_rows, table, dims, first, vmem=62):
    stations, pols, spec, taps, group, chans, counts = dims
    nsel = table.shape[0] // 2
    size = pols * 2 * stations
    rows = v.shape[1]
    return pl.pallas_call(
        functools.partial(channelize_kernel, dims),
        grid=(stations,),
        out_shape=[pltpu.HBM((chans, count * size, LANES), jnp.bfloat16) for count in counts],
        in_specs=[
            pl.BlockSpec((1, rows, LANES), lambda s: (s + first, 0, 0)),
            pl.BlockSpec(taps_rows.shape, lambda s: (0, 0)),
            pl.BlockSpec(table.shape, lambda s: (0, 0)),
        ],
        out_specs=[pl.BlockSpec((chans, count * size, LANES), lambda s: (0, 0, 0)) for count in counts],
        scratch_shapes=[
            pltpu.VMEM((spec * rows // (spec + taps - 1), LANES), jnp.float32),
            pltpu.VMEM((nsel * size, LANES), jnp.float32),
        ],
        compiler_params=pltpu.CompilerParams(vmem_limit_bytes=vmem << 20),
        cost_estimate=pl.CostEstimate(
            flops=14 * 10**9 * stations // 16, bytes_accessed=stations * rows * 256, transcendentals=0
        ),
        name="channelize",
    )(v, taps_rows, table)


def beam_kernel(dims, me_ref, w_ref, *rest):
    sub, pr, halves, groups, aliased = dims
    xs = rest[: halves * groups]
    o_ref, wide, rhs, outw = rest[halves * groups + aliased :]
    chans, _, local, m = xs[0].shape
    local = local // pr
    stations = groups * chans * local * halves
    st_n = stations // LANES
    lines = st_n * 2
    me = me_ref[0]
    for d in range(groups):
        g = me ^ d
        for c in range(chans):
            low = pl.multiple_of((c * groups + g) * (local * halves), local * halves)
            for q in range(0, pr, 2):
                part = [
                    jnp.concatenate(
                        [xs[h * groups + d][c, 0, (q + r) * local : (q + r + 1) * local, :] for h in range(halves)], axis=0
                    )
                    for r in range(2)
                ]
                rhs[pl.ds(low, local * halves), q * m : (q + 1) * m] = part[0]
                rhs[pl.ds(low, local * halves), (q + 1) * m : (q + 2) * m] = part[1]
                rhs[pl.ds(stations + low, local * halves), q * m : (q + 1) * m] = -part[1]
                rhs[pl.ds(stations + low, local * halves), (q + 1) * m : (q + 2) * m] = part[0]
    beams = w_ref.shape[1] // lines
    tile = beams // sub
    right = rhs[...]
    for i in range(sub):
        wide[i] = w_ref[0, i * tile * lines : (i + 1) * tile * lines, :].astype(jnp.float32)
        left = jnp.concatenate(
            [
                wide[i, pl.ds(st * 2 + w, tile, stride=lines), :].astype(jnp.bfloat16)
                for w in range(2)
                for st in range(st_n)
            ],
            axis=1,
        )
        out = jnp.dot(left, right, preferred_element_type=jnp.float32)
        for q in range(pr):
            outw[i, pl.ds(q, tile, stride=pr), :] = out[:, q * m : (q + 1) * m]
        o_ref[0, i * tile * pr : (i + 1) * tile * pr, :] = outw[i].astype(jnp.bfloat16)


def form_beams(me, w, xs, lows, count, pr, halves, first, stations, so_far=None, sub=4):
    chans, _, local, m = xs[0].shape
    channels, rows = w.shape[:2]
    st_n = stations // LANES
    beams = rows // (2 * st_n)
    tile = beams // sub
    groups = len(xs) // halves
    aliased = so_far is not None
    operands = [me, w, *xs] + ([so_far] if aliased else [])
    return pl.pallas_call(
        functools.partial(beam_kernel, (sub, pr, halves, groups, int(aliased))),
        grid=(count,),
        out_shape=jax.ShapeDtypeStruct((channels, beams * pr, m), jnp.bfloat16),
        in_specs=[
            pl.BlockSpec(memory_space=pltpu.SMEM),
            pl.BlockSpec((1, rows, LANES), lambda j: (j + first, 0, 0)),
            *[
                pl.BlockSpec((chans, 1, local, m), functools.partial(lambda low, j: (0, j + low, 0, 0), low))
                for low in lows
            ],
            *([pl.BlockSpec(memory_space=pl.ANY)] if aliased else []),
        ],
        out_specs=pl.BlockSpec((1, beams * pr, m), lambda j: (j + first, 0, 0)),
        scratch_shapes=[
            pltpu.VMEM((sub, tile * st_n * 2, LANES), jnp.float32),
            pltpu.VMEM((2 * stations, pr * m), jnp.bfloat16),
            pltpu.VMEM((sub, tile * pr, m), jnp.float32),
        ],
        input_output_aliases={len(operands) - 1: 0} if aliased else {},
        compiler_params=pltpu.CompilerParams(vmem_limit_bytes=62 << 20),
        cost_estimate=pl.CostEstimate(
            flops=24 * 10**9 * count // 12, bytes_accessed=count * rows * 256, transcendentals=0
        ),
        name="beams",
    )(*operands)


def shards(voltages, filter_taps, chan_index, beam_weights):
    stations, pols, blocks, width = voltages.shape
    taps, fft_size = filter_taps.shape
    chans, groups = lax.axis_size("chan"), lax.axis_size("grp")
    mine, beams, parts, whole = beam_weights.shape
    spec = blocks - taps + 1
    tiles, pr, st_n = width // LANES, pols * 2, whole // LANES
    table = build_table(chan_index, fft_size)
    taps_rows = jnp.repeat(filter_taps.reshape(-1, LANES), pols, axis=0)
    v = voltages.transpose(0, 2, 1, 3).reshape(stations, blocks, pols, tiles, LANES)
    v = v.transpose(0, 1, 3, 2, 4).reshape(stations, blocks * tiles * pols, LANES)
    w = beam_weights.reshape(mine, beams, 2, st_n, LANES).transpose(0, 1, 3, 2, 4).reshape(mine, beams * st_n * 2, LANES)
    me = lax.axis_index("grp").astype(jnp.int32).reshape(1)

    if stations % 16:
        (spectra,) = channelize(v, taps_rows, table, (stations, pols, spec, taps, 8, chans, (mine,)), 0)
        turned = lax.all_to_all(spectra, "chan", split_axis=0, concat_axis=0, tiled=True)
        x = lax.all_gather(turned, "grp", axis=0, tiled=False)
        x = x.reshape(groups, chans, mine, pr, stations, spec).transpose(2, 3, 1, 0, 4, 5)
        x = x.reshape(1, mine, pr * whole, spec)
        out = form_beams(jnp.zeros_like(me), w, [x], [0], mine, pr, 1, 0, whole)
        return out.reshape(mine, beams, pols, 2, spec)

    local = stations // 2
    splits = ((mine,), COUNTS(mine))
    pieces = []
    for h, counts in enumerate(splits):
        spectra = channelize(v, taps_rows, table, (local, pols, spec, taps, GROUP, chans, counts), h * local)
        row, first = [], 0
        for part, count in zip(spectra, counts):
            turned = lax.all_to_all(part, "chan", split_axis=0, concat_axis=0, tiled=True)
            got = [turned] + [None] * (groups - 1)
            for d in range(2, groups, 2):
                got[d] = lax.ppermute(turned, "grp", [(g, g ^ d) for g in range(groups)])
            for d in range(0, groups, 2):
                got[d + 1] = lax.ppermute(got[d], "grp", [(g, g ^ 1) for g in range(groups)])
            row.append((first, count, [x.reshape(chans, count, pr * local, spec) for x in got]))
            first += count
        pieces.append(row)
    out = None
    for first, count, xs in pieces[1]:
        whole_xs = pieces[0][0][2]
        lows = [first] * groups + [0] * groups
        out = form_beams(me, w, whole_xs + xs, lows, count, pr, 2, first, whole, out)
    return out.reshape(mine, beams, pols, 2, spec)


GROUP = 16


def COUNTS(mine):
    return (mine // 2, mine - mine // 2)


def solution(mesh):
    placed = (P(("chan", "grp"), None, None, None), P(), P(), P("chan", "grp", None, None))
    return jax.shard_map(
        shards,
        mesh=mesh,
        in_specs=placed,
        out_specs=P("chan", "grp", None, None, None),
        check_vma=False,
    )
```

```python
import functools
import math

import jax
import jax.numpy as jnp
from jax import lax
from jax.experimental import pallas as pl
from jax.experimental.pallas import tpu as pltpu
from jax.sharding import PartitionSpec as P

LANES = 128


def build_table(chan_index, fft_size):
    position = jnp.arange(fft_size, dtype=jnp.int32)
    phase = chan_index[:, None] * position[None, :] % fft_size
    angle = 2.0 * math.pi / fft_size * phase.astype(jnp.float32)
    factor = 1.0 / math.sqrt(fft_size)
    cosine = jnp.cos(angle) * factor
    sine = jnp.sin(angle) * factor
    first = jnp.concatenate([cosine, sine], axis=1)
    second = jnp.concatenate([-sine, cosine], axis=1)
    return jnp.concatenate([first, second], axis=0).astype(jnp.bfloat16)


def channelize_kernel(dims, v_ref, t_ref, f_ref, *rest):
    stations, pols, spec, taps, group, split, chans, counts = dims
    outs, (tap_rows, fir, acc) = rest[: len(counts)], rest[len(counts) :]
    s = pl.program_id(0)
    tiles = v_ref.shape[1] // (spec + taps - 1) // pols
    lines = tiles * pols
    half = lines // 2
    nsel = f_ref.shape[0] // 2

    @pl.when(s == 0)
    def _():
        for t in range(taps):
            for n in range(half // pols):
                row = t_ref[t : t + 1, n * LANES : (n + 1) * LANES]
                tap_rows[t * half + n * pols : t * half + (n + 1) * pols, :] = jnp.broadcast_to(row, (pols, LANES))

    def filter_part(slot, low, high):
        tap = [tap_rows[t * half : (t + 1) * half, :] for t in range(taps)]
        for m0 in range(low, high, group):
            x = v_ref[0, m0 * lines : (m0 + group + taps - 1) * lines, :]
            x = x.astype(jnp.float32).reshape(group + taps - 1, 2, half, LANES)
            for h in range(2):
                for g in range(group):
                    total = x[g, h] * tap[0]
                    for t in range(1, taps):
                        total = total + x[g + t, h] * tap[t]
                    row = (m0 + g) * (lines + 1) + h * half
                    fir[slot, row : row + half, :] = total

    def transform_part(slot, n0, n1):
        rows = []
        for p in range(pols):
            cols = [fir[slot, pl.ds(n * pols + p, spec, stride=lines + 1), :].astype(jnp.bfloat16) for n in range(n0, n1)]
            rows.append(jnp.concatenate(cols, axis=1))
        return lax.dot_general(
            f_ref[:, n0 * LANES : n1 * LANES],
            jnp.concatenate(rows, axis=0),
            (((1,), (1,)), ((), ())),
            preferred_element_type=jnp.float32,
        )

    def store(out, station):
        for p in range(pols):
            turned = out[:, p * spec : (p + 1) * spec]
            for r in range(2):
                acc[pl.ds((p * 2 + r) * stations + station, nsel, stride=pols * 2 * stations + 1), :] = turned[
                    r * nsel : (r + 1) * nsel, :
                ]

    def both(slot, old, do_filter, do_transform):
        out = None
        for i in range(split):
            if do_transform:
                part = transform_part(old, i * tiles // split, (i + 1) * tiles // split)
                out = part if out is None else out + part
            if do_filter:
                filter_part(slot, i * spec // split, (i + 1) * spec // split)
        if do_transform:
            store(out, s - 1)

    @pl.when(s == 0)
    def _():
        both(0, 1, True, False)

    for parity in range(2):
        @pl.when((s > 0) & (s < stations) & (lax.rem(s, 2) == parity))
        def _(parity=parity):
            both(parity, 1 - parity, True, True)

    @pl.when(s == stations)
    def _():
        both(0, (stations - 1) % 2, False, True)
        size = pols * 2 * stations
        mine = nsel // chans
        for c in range(chans):
            k = c * mine
            for out_ref, count in zip(outs, counts):
                for j in range(count):
                    rows = acc[k * (size + 1) : k * (size + 1) + size, :]
                    out_ref[c, j * size : (j + 1) * size, :] = rows.astype(jnp.bfloat16)
                    k += 1


def channelize(v, filter_taps, table, dims, first):
    stations, pols, spec, taps, group, split, chans, counts = dims
    nsel = table.shape[0] // 2
    size = pols * 2 * stations
    rows = v.shape[1]
    lines = rows // (spec + taps - 1)
    return pl.pallas_call(
        functools.partial(channelize_kernel, dims),
        grid=(stations + 1,),
        out_shape=[pltpu.HBM((chans, count * size, LANES), jnp.bfloat16) for count in counts],
        in_specs=[
            pl.BlockSpec((1, rows, LANES), lambda s: (jnp.minimum(s, stations - 1) + first, 0, 0)),
            pl.BlockSpec(filter_taps.shape, lambda s: (0, 0)),
            pl.BlockSpec(table.shape, lambda s: (0, 0)),
        ],
        out_specs=[pl.BlockSpec((chans, count * size, LANES), lambda s: (0, 0, 0)) for count in counts],
        scratch_shapes=[
            pltpu.VMEM((taps * lines // 2, LANES), jnp.float32),
            pltpu.VMEM((2, spec * (lines + 1), LANES), jnp.float32),
            pltpu.VMEM((nsel * (size + 1), LANES), jnp.float32),
        ],
        compiler_params=pltpu.CompilerParams(vmem_limit_bytes=62 << 20),
        cost_estimate=pl.CostEstimate(flops=14 * 10**9 * stations // 16, bytes_accessed=stations * rows * 256, transcendentals=0),
        name="channelize",
    )(v, filter_taps, table)


def beam_kernel(dims, me_ref, w_ref, *rest):
    sub, pr, halves, groups, aliased = dims
    for k in range(w_ref.shape[0]):
        one_channel(k, sub, pr, halves, groups, me_ref, w_ref, rest[: halves * groups], *rest[halves * groups + aliased :])


def one_channel(k, sub, pr, halves, groups, me_ref, w_ref, xs, o_ref, wide, rhs, outw):
    chans, _, local, m = xs[0].shape
    local = local // pr
    stations = groups * chans * local * halves
    st_n = stations // LANES
    lines = st_n * 2
    me = me_ref[0]
    for d in range(groups):
        g = me ^ d
        for c in range(chans):
            low = pl.multiple_of((c * groups + g) * (local * halves), local * halves)
            for q in range(0, pr, 2):
                part = [
                    jnp.concatenate(
                        [xs[h * groups + d][c, k, (q + r) * local : (q + r + 1) * local, :] for h in range(halves)], axis=0
                    )
                    for r in range(2)
                ]
                rhs[k % 2, pl.ds(low, local * halves), q * m : (q + 1) * m] = part[0]
                rhs[k % 2, pl.ds(low, local * halves), (q + 1) * m : (q + 2) * m] = part[1]
                rhs[k % 2, pl.ds(stations + low, local * halves), q * m : (q + 1) * m] = -part[1]
                rhs[k % 2, pl.ds(stations + low, local * halves), (q + 1) * m : (q + 2) * m] = part[0]
    beams = w_ref.shape[1] // lines
    tile = beams // sub
    right = rhs[k % 2]
    for i in range(sub):
        for b in range(0, tile, 2):
            low = (i * tile + b) * lines
            pair = w_ref[k, low : low + 2 * lines, :].astype(jnp.float32)
            wide[i, b * (lines + 1) : b * (lines + 1) + lines, :] = pair[:lines]
            wide[i, (b + 1) * (lines + 1) : (b + 1) * (lines + 1) + lines, :] = pair[lines:]
        left = jnp.concatenate(
            [
                wide[i, pl.ds(st * 2 + w, tile, stride=lines + 1), :].astype(jnp.bfloat16)
                for w in range(2)
                for st in range(st_n)
            ],
            axis=1,
        )
        out = jnp.dot(left, right, preferred_element_type=jnp.float32)
        for q in range(pr):
            outw[i, pl.ds(q, tile, stride=pr), :] = out[:, q * m : (q + 1) * m]
        o_ref[k, i * tile * pr : (i + 1) * tile * pr, :] = outw[i].astype(jnp.bfloat16)


def form_beams(me, w, xs, lows, count, pr, halves, first, stations, so_far=None, sub=4, each=1):
    chans, _, local, m = xs[0].shape
    channels, rows = w.shape[:2]
    st_n = stations // LANES
    beams = rows // (2 * st_n)
    tile = beams // sub
    groups = len(xs) // halves
    aliased = so_far is not None
    operands = [me, w, *xs] + ([so_far] if aliased else [])
    return pl.pallas_call(
        functools.partial(beam_kernel, (sub, pr, halves, groups, int(aliased))),
        grid=(count // each,),
        out_shape=jax.ShapeDtypeStruct((channels, beams * pr, m), jnp.bfloat16),
        in_specs=[
            pl.BlockSpec(memory_space=pltpu.SMEM),
            pl.BlockSpec((each, rows, LANES), lambda j: (j + first // each, 0, 0)),
            *[
                pl.BlockSpec((chans, each, local, m), functools.partial(lambda low, j: (0, j + low, 0, 0), low // each))
                for low in lows
            ],
            *([pl.BlockSpec(memory_space=pl.ANY)] if aliased else []),
        ],
        out_specs=pl.BlockSpec((each, beams * pr, m), lambda j: (j + first // each, 0, 0)),
        scratch_shapes=[
            pltpu.VMEM((sub, tile * (st_n * 2 + 1), LANES), jnp.float32),
            pltpu.VMEM((2, 2 * stations, pr * m), jnp.bfloat16),
            pltpu.VMEM((sub, tile * pr, m), jnp.float32),
        ],
        input_output_aliases={len(operands) - 1: 0} if aliased else {},
        compiler_params=pltpu.CompilerParams(vmem_limit_bytes=62 << 20),
        cost_estimate=pl.CostEstimate(
            flops=24 * 10**9 * count // 12, bytes_accessed=count * rows * 256, transcendentals=0
        ),
        name="beams",
    )(*operands)


def shards(voltages, filter_taps, chan_index, beam_weights):
    stations, pols, blocks, width = voltages.shape
    taps, fft_size = filter_taps.shape
    chans, groups = lax.axis_size("chan"), lax.axis_size("grp")
    mine, beams, parts, whole = beam_weights.shape
    spec = blocks - taps + 1
    tiles, pr, st_n = width // LANES, pols * 2, whole // LANES
    table = build_table(chan_index, fft_size)
    v = voltages.transpose(0, 2, 1, 3).reshape(stations, blocks, pols, tiles, LANES)
    v = v.transpose(0, 1, 3, 2, 4).reshape(stations, blocks * tiles * pols, LANES)
    w = beam_weights.reshape(mine, beams, 2, st_n, LANES).transpose(0, 1, 3, 2, 4).reshape(mine, beams * st_n * 2, LANES)
    me = lax.axis_index("grp").astype(jnp.int32).reshape(1)

    if stations % 16:
        (spectra,) = channelize(v, filter_taps, table, (stations, pols, spec, taps, 16, 4, chans, (mine,)), 0)
        turned = lax.all_to_all(spectra, "chan", split_axis=0, concat_axis=0, tiled=True)
        x = lax.all_gather(turned, "grp", axis=0, tiled=False)
        x = x.reshape(groups, chans, mine, pr, stations, spec).transpose(2, 3, 1, 0, 4, 5)
        x = x.reshape(1, mine, pr * whole, spec)
        out = form_beams(jnp.zeros_like(me), w, [x], [0], mine, pr, 1, 0, whole)
        return out.reshape(mine, beams, pols, 2, spec)

    local = stations // 2
    counts = COUNTS(mine)
    first_half, second_half = [
        channelize(v, filter_taps, table, (local, pols, spec, taps, 16, 4, chans, part), h * local)
        for h, part in enumerate(((mine,), counts))
    ]

    def turn(part):
        return lax.all_to_all(part, "chan", split_axis=0, concat_axis=0, tiled=True)

    def far(part):
        return {d: lax.ppermute(part, "grp", [(g, g ^ d) for g in range(groups)]) for d in range(2, groups, 2)}

    def near(part):
        return lax.ppermute(part, "grp", [(g, g ^ 1) for g in range(groups)])

    def pairs(own, others):
        return [x.reshape(chans, -1, pr * local, spec) for x in (own, near(own))] + others

    def spread(others):
        return [y.reshape(chans, -1, pr * local, spec) for x in others.values() for y in (x, near(x))]

    def beams_of(xs, i, out):
        first, size = sum(counts[:i]), counts[i]
        each = EACH if size % EACH == 0 and first % EACH == 0 else 1
        return form_beams(me, w, early + xs, [first] * groups + [0] * groups, size, pr, 2, first, whole, out, each=each)

    tie = lax.optimization_barrier
    turned = turn(first_half[0])
    turned, second_half = tie((turned, second_half))
    far_0 = far(turned)
    turned_a = turn(second_half[0])
    far_a = far(turned_a)
    turned_b = turn(second_half[1])
    far_0, far_a, turned_b = tie((far_0, far_a, turned_b))
    far_b = far(turned_b)
    early = pairs(turned, spread(far_0))
    out = beams_of(pairs(turned_a, spread(far_a)), 0, None)
    far_b, out = tie((far_b, out))
    out = beams_of(pairs(turned_b, spread(far_b)), 1, out)
    return out.reshape(mine, beams, pols, 2, spec)


EACH = 2


def COUNTS(mine):
    a = mine // 4 * 2
    return (a, mine - a)


def solution(mesh):
    placed = (P(("chan", "grp"), None, None, None), P(), P(), P("chan", "grp", None, None))
    return jax.shard_map(
        shards,
        mesh=mesh,
        in_specs=placed,
        out_specs=P("chan", "grp", None, None, None),
        check_vma=False,
    )
```

```python
import functools
import math

import jax
import jax.numpy as jnp
from jax import lax
from jax.experimental import pallas as pl
from jax.experimental.pallas import tpu as pltpu
from jax.sharding import PartitionSpec as P

LANES = 128


def write_table(chan_ref, index_ref, f_ref):
    nsel, fft_size = f_ref.shape[0] // 2, f_ref.shape[1] // 2
    for k in range(nsel):
        index_ref[k : k + 1, :] = jnp.full((1, LANES), chan_ref[k], jnp.int32)
    index = index_ref[...]
    lane = lax.broadcasted_iota(jnp.int32, (nsel, LANES), 1)

    def parts(position):
        phase = lax.rem(index * position, fft_size)
        angle = 2.0 * math.pi / fft_size * phase.astype(jnp.float32)
        return jnp.cos(angle), jnp.sin(angle)

    factor = 1.0 / math.sqrt(fft_size)
    low_cos, low_sin = [x * factor for x in parts(lane)]
    high_cos, high_sin = parts(lax.rem(lane * LANES, fft_size))
    for h in range(fft_size // LANES):
        c = jnp.broadcast_to(high_cos[:, h : h + 1], (nsel, LANES))
        s = jnp.broadcast_to(high_sin[:, h : h + 1], (nsel, LANES))
        cosine = (c * low_cos - s * low_sin).astype(jnp.bfloat16)
        sine = (s * low_cos + c * low_sin).astype(jnp.bfloat16)
        real, imag = h * LANES, fft_size + h * LANES
        f_ref[:nsel, real : real + LANES] = cosine
        f_ref[:nsel, imag : imag + LANES] = sine
        f_ref[nsel:, real : real + LANES] = -sine
        f_ref[nsel:, imag : imag + LANES] = cosine


def channelize_kernel(dims, v_ref, t_ref, chan_ref, *rest):
    stations, pols, spec, taps, group, split, chans, counts = dims
    outs, (index_ref, f_ref, tap_rows, fir, acc) = rest[: len(counts)], rest[len(counts) :]
    s = pl.program_id(0)
    tiles = v_ref.shape[1] // (spec + taps - 1) // pols
    lines = tiles * pols
    half = lines // 2
    nsel = f_ref.shape[0] // 2

    @pl.when(s == 0)
    def _():
        write_table(chan_ref, index_ref, f_ref)
        for t in range(taps):
            for n in range(half // pols):
                row = t_ref[t : t + 1, n * LANES : (n + 1) * LANES]
                tap_rows[t * half + n * pols : t * half + (n + 1) * pols, :] = jnp.broadcast_to(row, (pols, LANES))

    def filter_part(slot, low, high):
        tap = [tap_rows[t * half : (t + 1) * half, :] for t in range(taps)]
        for m0 in range(low, high, group):
            x = v_ref[0, m0 * lines : (m0 + group + taps - 1) * lines, :]
            x = x.astype(jnp.float32).reshape(group + taps - 1, 2, half, LANES)
            for h in range(2):
                for g in range(group):
                    total = x[g, h] * tap[0]
                    for t in range(1, taps):
                        total = total + x[g + t, h] * tap[t]
                    row = (m0 + g) * (lines + 1) + h * half
                    fir[slot, row : row + half, :] = total

    def transform_part(slot, n0, n1):
        rows = []
        for p in range(pols):
            cols = [fir[slot, pl.ds(n * pols + p, spec, stride=lines + 1), :].astype(jnp.bfloat16) for n in range(n0, n1)]
            rows.append(jnp.concatenate(cols, axis=1))
        return lax.dot_general(
            f_ref[:, n0 * LANES : n1 * LANES],
            jnp.concatenate(rows, axis=0),
            (((1,), (1,)), ((), ())),
            preferred_element_type=jnp.float32,
        )

    def store(out, station):
        for p in range(pols):
            turned = out[:, p * spec : (p + 1) * spec]
            for r in range(2):
                acc[pl.ds((p * 2 + r) * stations + station, nsel, stride=pols * 2 * stations + 1), :] = turned[
                    r * nsel : (r + 1) * nsel, :
                ]

    def both(slot, old, do_filter, do_transform):
        out = None
        for i in range(split):
            if do_transform:
                part = transform_part(old, i * tiles // split, (i + 1) * tiles // split)
                out = part if out is None else out + part
            if do_filter:
                filter_part(slot, i * spec // split, (i + 1) * spec // split)
        if do_transform:
            store(out, s - 1)

    @pl.when(s == 0)
    def _():
        both(0, 1, True, False)

    for parity in range(2):
        @pl.when((s > 0) & (s < stations) & (lax.rem(s, 2) == parity))
        def _(parity=parity):
            both(parity, 1 - parity, True, True)

    @pl.when(s == stations)
    def _():
        both(0, (stations - 1) % 2, False, True)
        size = pols * 2 * stations
        mine = nsel // chans
        for c in range(chans):
            k = c * mine
            for out_ref, count in zip(outs, counts):
                for j in range(count):
                    rows = acc[k * (size + 1) : k * (size + 1) + size, :]
                    out_ref[c, j * size : (j + 1) * size, :] = rows.astype(jnp.bfloat16)
                    k += 1


def channelize(v, filter_taps, chan_index, dims, first):
    stations, pols, spec, taps, group, split, chans, counts = dims
    nsel = chan_index.shape[0]
    size = pols * 2 * stations
    rows = v.shape[1]
    lines = rows // (spec + taps - 1)
    return pl.pallas_call(
        functools.partial(channelize_kernel, dims),
        grid=(stations + 1,),
        out_shape=[pltpu.HBM((chans, count * size, LANES), jnp.bfloat16) for count in counts],
        in_specs=[
            pl.BlockSpec((1, rows, LANES), lambda s: (jnp.minimum(s, stations - 1) + first, 0, 0)),
            pl.BlockSpec(filter_taps.shape, lambda s: (0, 0)),
            pl.BlockSpec(memory_space=pltpu.SMEM),
        ],
        out_specs=[pl.BlockSpec((chans, count * size, LANES), lambda s: (0, 0, 0)) for count in counts],
        scratch_shapes=[
            pltpu.VMEM((nsel, LANES), jnp.int32),
            pltpu.VMEM((2 * nsel, 2 * filter_taps.shape[1]), jnp.bfloat16),
            pltpu.VMEM((taps * lines // 2, LANES), jnp.float32),
            pltpu.VMEM((2, (spec + 2) * (lines + 1), LANES), jnp.float32),
            pltpu.VMEM(((nsel + 2) * (size + 1), LANES), jnp.float32),
        ],
        compiler_params=pltpu.CompilerParams(vmem_limit_bytes=62 << 20),
        cost_estimate=pl.CostEstimate(flops=14 * 10**9 * stations // 16, bytes_accessed=stations * rows * 256, transcendentals=0),
        name="channelize",
    )(v, filter_taps, chan_index)


def beam_kernel(dims, me_ref, w_ref, *rest):
    sub, pr, halves, groups, aliased = dims
    for k in range(w_ref.shape[0]):
        one_channel(k, sub, pr, halves, groups, me_ref, w_ref, rest[: halves * groups], *rest[halves * groups + aliased :])


def one_channel(k, sub, pr, halves, groups, me_ref, w_ref, xs, o_ref, wide, rhs, outw):
    chans, _, local, m = xs[0].shape
    local = local // pr
    stations = groups * chans * local * halves
    st_n = stations // LANES
    lines = st_n * 2
    me = me_ref[0]
    for d in range(groups):
        g = me ^ d
        for c in range(chans):
            low = pl.multiple_of((c * groups + g) * (local * halves), local * halves)
            for q in range(0, pr, 2):
                part = [
                    jnp.concatenate(
                        [xs[h * groups + d][c, k, (q + r) * local : (q + r + 1) * local, :] for h in range(halves)], axis=0
                    )
                    for r in range(2)
                ]
                rhs[k % 2, pl.ds(low, local * halves), q * m : (q + 1) * m] = part[0]
                rhs[k % 2, pl.ds(low, local * halves), (q + 1) * m : (q + 2) * m] = part[1]
                rhs[k % 2, pl.ds(stations + low, local * halves), q * m : (q + 1) * m] = -part[1]
                rhs[k % 2, pl.ds(stations + low, local * halves), (q + 1) * m : (q + 2) * m] = part[0]
    beams = w_ref.shape[1] // lines
    tile = beams // sub
    right = rhs[k % 2]
    for i in range(sub):
        for b in range(0, tile, 2):
            low = (i * tile + b) * lines
            pair = w_ref[k, low : low + 2 * lines, :].astype(jnp.float32)
            wide[i, b * (lines + 1) : b * (lines + 1) + lines, :] = pair[:lines]
            wide[i, (b + 1) * (lines + 1) : (b + 1) * (lines + 1) + lines, :] = pair[lines:]
        left = jnp.concatenate(
            [
                wide[i, pl.ds(st * 2 + w, tile, stride=lines + 1), :].astype(jnp.bfloat16)
                for w in range(2)
                for st in range(st_n)
            ],
            axis=1,
        )
        out = jnp.dot(left, right, preferred_element_type=jnp.float32)
        for q in range(pr):
            outw[i, pl.ds(q, tile, stride=pr), :] = out[:, q * m : (q + 1) * m]
        o_ref[k, i * tile * pr : (i + 1) * tile * pr, :] = outw[i, : tile * pr, :].astype(jnp.bfloat16)


def form_beams(me, w, xs, lows, count, pr, halves, first, stations, so_far=None, sub=4, each=1):
    chans, _, local, m = xs[0].shape
    channels, rows = w.shape[:2]
    st_n = stations // LANES
    beams = rows // (2 * st_n)
    tile = beams // sub
    groups = len(xs) // halves
    aliased = so_far is not None
    operands = [me, w, *xs] + ([so_far] if aliased else [])
    return pl.pallas_call(
        functools.partial(beam_kernel, (sub, pr, halves, groups, int(aliased))),
        grid=(count // each,),
        out_shape=jax.ShapeDtypeStruct((channels, beams * pr, m), jnp.bfloat16),
        in_specs=[
            pl.BlockSpec(memory_space=pltpu.SMEM),
            pl.BlockSpec((each, rows, LANES), lambda j: (j + first // each, 0, 0)),
            *[
                pl.BlockSpec((chans, each, local, m), functools.partial(lambda low, j: (0, j + low, 0, 0), low // each))
                for low in lows
            ],
            *([pl.BlockSpec(memory_space=pl.ANY)] if aliased else []),
        ],
        out_specs=pl.BlockSpec((each, beams * pr, m), lambda j: (j + first // each, 0, 0)),
        scratch_shapes=[
            pltpu.VMEM((sub, (tile + 8) * (st_n * 2 + 1), LANES), jnp.float32),
            pltpu.VMEM((2, 2 * stations, pr * m), jnp.bfloat16),
            pltpu.VMEM((sub, (tile + 8) * pr, m), jnp.float32),
        ],
        input_output_aliases={len(operands) - 1: 0} if aliased else {},
        compiler_params=pltpu.CompilerParams(vmem_limit_bytes=62 << 20),
        cost_estimate=pl.CostEstimate(
            flops=24 * 10**9 * count // 12, bytes_accessed=count * rows * 256, transcendentals=0
        ),
        name="beams",
    )(*operands)


def shards(voltages, filter_taps, chan_index, beam_weights):
    stations, pols, blocks, width = voltages.shape
    taps, fft_size = filter_taps.shape
    chans, groups = lax.axis_size("chan"), lax.axis_size("grp")
    mine, beams, parts, whole = beam_weights.shape
    spec = blocks - taps + 1
    tiles, pr, st_n = width // LANES, pols * 2, whole // LANES
    v = voltages.transpose(0, 2, 1, 3).reshape(stations, blocks, pols, tiles, LANES)
    v = v.transpose(0, 1, 3, 2, 4).reshape(stations, blocks * tiles * pols, LANES)
    w = beam_weights.reshape(mine, beams, 2, st_n, LANES).transpose(0, 1, 3, 2, 4).reshape(mine, beams * st_n * 2, LANES)
    me = lax.axis_index("grp").astype(jnp.int32).reshape(1)

    if stations % 16:
        (spectra,) = channelize(v, filter_taps, chan_index, (stations, pols, spec, taps, 16, 4, chans, (mine,)), 0)
        turned = lax.all_to_all(spectra, "chan", split_axis=0, concat_axis=0, tiled=True)
        x = lax.all_gather(turned, "grp", axis=0, tiled=False)
        x = x.reshape(groups, chans, mine, pr, stations, spec).transpose(2, 3, 1, 0, 4, 5)
        x = x.reshape(1, mine, pr * whole, spec)
        out = form_beams(jnp.zeros_like(me), w, [x], [0], mine, pr, 1, 0, whole)
        return out.reshape(mine, beams, pols, 2, spec)

    local = stations // 2
    counts = COUNTS(mine)
    first_half, second_half = [
        channelize(v, filter_taps, chan_index, (local, pols, spec, taps, 16, 4, chans, part), h * local)
        for h, part in enumerate(((mine,), counts))
    ]

    def turn(part):
        return lax.all_to_all(part, "chan", split_axis=0, concat_axis=0, tiled=True)

    def far(part):
        return {d: lax.ppermute(part, "grp", [(g, g ^ d) for g in range(groups)]) for d in range(2, groups, 2)}

    def near(part):
        return lax.ppermute(part, "grp", [(g, g ^ 1) for g in range(groups)])

    def pairs(own, others):
        return [x.reshape(chans, -1, pr * local, spec) for x in (own, near(own))] + others

    def spread(others):
        return [y.reshape(chans, -1, pr * local, spec) for x in others.values() for y in (x, near(x))]

    def beams_of(xs, i, out):
        first, size = sum(counts[:i]), counts[i]
        each = EACH if size % EACH == 0 and first % EACH == 0 else 1
        return form_beams(me, w, early + xs, [first] * groups + [0] * groups, size, pr, 2, first, whole, out, each=each)

    tie = lax.optimization_barrier
    turned = turn(first_half[0])
    turned, second_half = tie((turned, second_half))
    far_0 = far(turned)
    turned_a = turn(second_half[0])
    far_a = far(turned_a)
    turned_b = turn(second_half[1])
    far_a, turned_b = tie((far_a, turned_b))
    far_b = far(turned_b)
    early = pairs(turned, spread(far_0))
    out = beams_of(pairs(turned_a, spread(far_a)), 0, None)
    far_b, out = tie((far_b, out))
    out = beams_of(pairs(turned_b, spread(far_b)), 1, out)
    return out.reshape(mine, beams, pols, 2, spec)


EACH = 2


def COUNTS(mine):
    a = mine // 4 * 2
    return (a, mine - a)


def solution(mesh):
    placed = (P(("chan", "grp"), None, None, None), P(), P(), P("chan", "grp", None, None))
    return jax.shard_map(
        shards,
        mesh=mesh,
        in_specs=placed,
        out_specs=P("chan", "grp", None, None, None),
        check_vma=False,
    )
```

```python
import functools
import math

import jax
import jax.numpy as jnp
from jax import lax
from jax.experimental import pallas as pl
from jax.experimental.pallas import tpu as pltpu
from jax.sharding import PartitionSpec as P

LANES = 128


def write_table(chan_ref, index_ref, f_ref):
    nsel, fft_size = f_ref.shape[0] // 2, f_ref.shape[1] // 2
    for k in range(nsel):
        index_ref[k : k + 1, :] = jnp.full((1, LANES), chan_ref[k], jnp.int32)
    index = index_ref[...]
    lane = lax.broadcasted_iota(jnp.int32, (nsel, LANES), 1)

    def parts(position):
        phase = lax.rem(index * position, fft_size)
        angle = 2.0 * math.pi / fft_size * phase.astype(jnp.float32)
        return jnp.cos(angle), jnp.sin(angle)

    factor = 1.0 / math.sqrt(fft_size)
    low_cos, low_sin = [x * factor for x in parts(lane)]
    high_cos, high_sin = parts(lax.rem(lane * LANES, fft_size))
    for h in range(fft_size // LANES):
        c = jnp.broadcast_to(high_cos[:, h : h + 1], (nsel, LANES))
        s = jnp.broadcast_to(high_sin[:, h : h + 1], (nsel, LANES))
        cosine = (c * low_cos - s * low_sin).astype(jnp.bfloat16)
        sine = (s * low_cos + c * low_sin).astype(jnp.bfloat16)
        real, imag = h * LANES, fft_size + h * LANES
        f_ref[:nsel, real : real + LANES] = cosine
        f_ref[:nsel, imag : imag + LANES] = sine
        f_ref[nsel:, real : real + LANES] = -sine
        f_ref[nsel:, imag : imag + LANES] = cosine


def channelize_kernel(dims, v_ref, t_ref, chan_ref, *rest):
    stations, pols, spec, taps, group, split, chans, counts = dims
    outs, (index_ref, f_ref, tap_rows, fir, acc) = rest[: len(counts)], rest[len(counts) :]
    s = pl.program_id(0)
    tiles = v_ref.shape[1] // (spec + taps - 1) // pols
    lines = tiles * pols
    half = lines // 2
    nsel = f_ref.shape[0] // 2

    @pl.when(s == 0)
    def _():
        write_table(chan_ref, index_ref, f_ref)
        for t in range(taps):
            for n in range(half // pols):
                row = t_ref[t : t + 1, n * LANES : (n + 1) * LANES]
                tap_rows[t * half + n * pols : t * half + (n + 1) * pols, :] = jnp.broadcast_to(row, (pols, LANES))

    def filter_part(slot, low, high):
        tap = [tap_rows[t * half : (t + 1) * half, :] for t in range(taps)]
        for m0 in range(low, high, group):
            x = v_ref[0, m0 * lines : (m0 + group + taps - 1) * lines, :]
            x = x.astype(jnp.float32).reshape(group + taps - 1, 2, half, LANES)
            for h in range(2):
                for g in range(group):
                    total = x[g, h] * tap[0]
                    for t in range(1, taps):
                        total = total + x[g + t, h] * tap[t]
                    row = (m0 + g) * (lines + 1) + h * half
                    fir[slot, row : row + half, :] = total

    def transform_part(slot, n0, n1):
        rows = []
        for p in range(pols):
            cols = [fir[slot, pl.ds(n * pols + p, spec, stride=lines + 1), :].astype(jnp.bfloat16) for n in range(n0, n1)]
            rows.append(jnp.concatenate(cols, axis=1))
        return lax.dot_general(
            f_ref[:, n0 * LANES : n1 * LANES],
            jnp.concatenate(rows, axis=0),
            (((1,), (1,)), ((), ())),
            preferred_element_type=jnp.float32,
        )

    def store(out, station):
        for p in range(pols):
            turned = out[:, p * spec : (p + 1) * spec]
            for r in range(2):
                acc[pl.ds((p * 2 + r) * stations + station, nsel, stride=pols * 2 * stations + 1), :] = turned[
                    r * nsel : (r + 1) * nsel, :
                ]

    def both(slot, old, do_filter, do_transform):
        out = None
        for i in range(split):
            if do_transform:
                part = transform_part(old, i * tiles // split, (i + 1) * tiles // split)
                out = part if out is None else out + part
            if do_filter:
                filter_part(slot, i * spec // split, (i + 1) * spec // split)
        if do_transform:
            store(out, s - 1)

    @pl.when(s == 0)
    def _():
        both(0, 1, True, False)

    for parity in range(2):
        @pl.when((s > 0) & (s < stations) & (lax.rem(s, 2) == parity))
        def _(parity=parity):
            both(parity, 1 - parity, True, True)

    @pl.when(s == stations)
    def _():
        both(0, (stations - 1) % 2, False, True)
        size = pols * 2 * stations
        mine = nsel // chans
        for c in range(chans):
            k = c * mine
            for out_ref, count in zip(outs, counts):
                for j in range(count):
                    rows = acc[k * (size + 1) : k * (size + 1) + size, :]
                    out_ref[c, j * size : (j + 1) * size, :] = rows.astype(jnp.bfloat16)
                    k += 1


def channelize(v, filter_taps, chan_index, dims, first):
    stations, pols, spec, taps, group, split, chans, counts = dims
    nsel = chan_index.shape[0]
    size = pols * 2 * stations
    rows = v.shape[1]
    lines = rows // (spec + taps - 1)
    return pl.pallas_call(
        functools.partial(channelize_kernel, dims),
        grid=(stations + 1,),
        out_shape=[pltpu.HBM((chans, count * size, LANES), jnp.bfloat16) for count in counts],
        in_specs=[
            pl.BlockSpec((1, rows, LANES), lambda s: (jnp.minimum(s, stations - 1) + first, 0, 0)),
            pl.BlockSpec(filter_taps.shape, lambda s: (0, 0)),
            pl.BlockSpec(memory_space=pltpu.SMEM),
        ],
        out_specs=[pl.BlockSpec((chans, count * size, LANES), lambda s: (0, 0, 0)) for count in counts],
        scratch_shapes=[
            pltpu.VMEM((nsel, LANES), jnp.int32),
            pltpu.VMEM((2 * nsel, 2 * filter_taps.shape[1]), jnp.bfloat16),
            pltpu.VMEM((taps * lines // 2, LANES), jnp.float32),
            pltpu.VMEM((2, (spec + 2) * (lines + 1), LANES), jnp.float32),
            pltpu.VMEM(((nsel + 2) * (size + 1), LANES), jnp.float32),
        ],
        compiler_params=pltpu.CompilerParams(vmem_limit_bytes=62 << 20),
        cost_estimate=pl.CostEstimate(flops=14 * 10**9 * stations // 16, bytes_accessed=stations * rows * 256, transcendentals=0),
        name="channelize",
    )(v, filter_taps, chan_index)


def beam_kernel(dims, me_ref, w_ref, *rest):
    sub, pr, halves, groups, aliased = dims
    for k in range(w_ref.shape[0]):
        one_channel(k, sub, pr, halves, groups, me_ref, w_ref, rest[: halves * groups], *rest[halves * groups + aliased :])


def one_channel(k, sub, pr, halves, groups, me_ref, w_ref, xs, o_ref, wide, rhs, outw):
    chans, _, local, m = xs[0].shape
    local = local // pr
    stations = groups * chans * local * halves
    st_n = stations // LANES
    lines = st_n * 2
    me = me_ref[0]
    for d in range(groups):
        g = me ^ d
        for c in range(chans):
            low = pl.multiple_of((c * groups + g) * (local * halves), local * halves)
            for q in range(0, pr, 2):
                part = [
                    jnp.concatenate(
                        [xs[h * groups + d][c, k, (q + r) * local : (q + r + 1) * local, :] for h in range(halves)], axis=0
                    )
                    for r in range(2)
                ]
                rhs[k % 2, pl.ds(low, local * halves), q * m : (q + 1) * m] = part[0]
                rhs[k % 2, pl.ds(low, local * halves), (q + 1) * m : (q + 2) * m] = part[1]
                rhs[k % 2, pl.ds(stations + low, local * halves), q * m : (q + 1) * m] = -part[1]
                rhs[k % 2, pl.ds(stations + low, local * halves), (q + 1) * m : (q + 2) * m] = part[0]
    beams = w_ref.shape[1] // lines
    tile = beams // sub
    right = rhs[k % 2]
    for i in range(sub):
        for b in range(0, tile, 2):
            low = (i * tile + b) * lines
            pair = w_ref[k, low : low + 2 * lines, :].astype(jnp.float32)
            wide[i, b * (lines + 1) : b * (lines + 1) + lines, :] = pair[:lines]
            wide[i, (b + 1) * (lines + 1) : (b + 1) * (lines + 1) + lines, :] = pair[lines:]
        left = jnp.concatenate(
            [
                wide[i, pl.ds(st * 2 + w, tile, stride=lines + 1), :].astype(jnp.bfloat16)
                for w in range(2)
                for st in range(st_n)
            ],
            axis=1,
        )
        out = jnp.dot(left, right, preferred_element_type=jnp.float32)
        for q in range(pr):
            outw[i, pl.ds(q, tile, stride=pr), :] = out[:, q * m : (q + 1) * m]
        o_ref[k, i * tile * pr : (i + 1) * tile * pr, :] = outw[i, : tile * pr, :].astype(jnp.bfloat16)


def form_beams(me, w, xs, lows, count, pr, halves, first, stations, so_far=None, sub=4, each=1):
    chans, _, local, m = xs[0].shape
    channels, rows = w.shape[:2]
    st_n = stations // LANES
    beams = rows // (2 * st_n)
    tile = beams // sub
    groups = len(xs) // halves
    aliased = so_far is not None
    operands = [me, w, *xs] + ([so_far] if aliased else [])
    return pl.pallas_call(
        functools.partial(beam_kernel, (sub, pr, halves, groups, int(aliased))),
        grid=(count // each,),
        out_shape=jax.ShapeDtypeStruct((channels, beams * pr, m), jnp.bfloat16),
        in_specs=[
            pl.BlockSpec(memory_space=pltpu.SMEM),
            pl.BlockSpec((each, rows, LANES), lambda j: (j + first // each, 0, 0)),
            *[
                pl.BlockSpec((chans, each, local, m), functools.partial(lambda low, j: (0, j + low, 0, 0), low // each))
                for low in lows
            ],
            *([pl.BlockSpec(memory_space=pl.ANY)] if aliased else []),
        ],
        out_specs=pl.BlockSpec((each, beams * pr, m), lambda j: (j + first // each, 0, 0)),
        scratch_shapes=[
            pltpu.VMEM((sub, (tile + 8) * (st_n * 2 + 1), LANES), jnp.float32),
            pltpu.VMEM((2, 2 * stations, pr * m), jnp.bfloat16),
            pltpu.VMEM((sub, (tile + 8) * pr, m), jnp.float32),
        ],
        input_output_aliases={len(operands) - 1: 0} if aliased else {},
        compiler_params=pltpu.CompilerParams(vmem_limit_bytes=40 << 20),
        cost_estimate=pl.CostEstimate(
            flops=24 * 10**9 * count // 12, bytes_accessed=count * rows * 256, transcendentals=0
        ),
        name="beams",
    )(*operands)


def shards(voltages, filter_taps, chan_index, beam_weights):
    stations, pols, blocks, width = voltages.shape
    taps, fft_size = filter_taps.shape
    chans, groups = lax.axis_size("chan"), lax.axis_size("grp")
    mine, beams, parts, whole = beam_weights.shape
    spec = blocks - taps + 1
    tiles, pr, st_n = width // LANES, pols * 2, whole // LANES
    v = voltages.transpose(0, 2, 1, 3).reshape(stations, blocks, pols, tiles, LANES)
    v = v.transpose(0, 1, 3, 2, 4).reshape(stations, blocks * tiles * pols, LANES)
    w = beam_weights.reshape(mine, beams, 2, st_n, LANES).transpose(0, 1, 3, 2, 4).reshape(mine, beams * st_n * 2, LANES)
    me = lax.axis_index("grp").astype(jnp.int32).reshape(1)

    if stations % 16:
        (spectra,) = channelize(v, filter_taps, chan_index, (stations, pols, spec, taps, 16, 4, chans, (mine,)), 0)
        turned = lax.all_to_all(spectra, "chan", split_axis=0, concat_axis=0, tiled=True)
        x = lax.all_gather(turned, "grp", axis=0, tiled=False)
        x = x.reshape(groups, chans, mine, pr, stations, spec).transpose(2, 3, 1, 0, 4, 5)
        x = x.reshape(1, mine, pr * whole, spec)
        out = form_beams(jnp.zeros_like(me), w, [x], [0], mine, pr, 1, 0, whole)
        return out.reshape(mine, beams, pols, 2, spec)

    local = stations // 2
    counts = COUNTS(mine)
    first_half, second_half = [
        channelize(v, filter_taps, chan_index, (local, pols, spec, taps, 16, 4, chans, part), h * local)
        for h, part in enumerate(((mine,), counts))
    ]

    def turn(part):
        return lax.all_to_all(part, "chan", split_axis=0, concat_axis=0, tiled=True)

    def far(part):
        return {d: lax.ppermute(part, "grp", [(g, g ^ d) for g in range(groups)]) for d in range(2, groups, 2)}

    def near(part):
        return lax.ppermute(part, "grp", [(g, g ^ 1) for g in range(groups)])

    def pairs(own, others):
        return [x.reshape(chans, -1, pr * local, spec) for x in (own, near(own))] + others

    def spread(others):
        return [y.reshape(chans, -1, pr * local, spec) for x in others.values() for y in (x, near(x))]

    def beams_of(xs, i, out):
        first, size = sum(counts[:i]), counts[i]
        each = EACH if size % EACH == 0 and first % EACH == 0 else 1
        return form_beams(me, w, early + xs, [first] * groups + [0] * groups, size, pr, 2, first, whole, out, each=each)

    tie = lax.optimization_barrier
    turned = turn(first_half[0])
    turned, second_half = tie((turned, second_half))
    far_0 = far(turned)
    turned_a = turn(second_half[0])
    far_a = far(turned_a)
    turned_b = turn(second_half[1])
    far_a, turned_b = tie((far_a, turned_b))
    far_b = far(turned_b)
    early = pairs(turned, spread(far_0))
    out = beams_of(pairs(turned_a, spread(far_a)), 0, None)
    far_b, out = tie((far_b, out))
    out = beams_of(pairs(turned_b, spread(far_b)), 1, out)
    return out.reshape(mine, beams, pols, 2, spec)


EACH = 2


def COUNTS(mine):
    a = mine // 4 * 2
    return (a, mine - a)


def solution(mesh):
    placed = (P(("chan", "grp"), None, None, None), P(), P(), P("chan", "grp", None, None))
    return jax.shard_map(
        shards,
        mesh=mesh,
        in_specs=placed,
        out_specs=P("chan", "grp", None, None, None),
        check_vma=False,
    )
```

```python
import functools
import math

import jax
import jax.numpy as jnp
from jax import lax
from jax.experimental import pallas as pl
from jax.experimental.pallas import tpu as pltpu
from jax.sharding import PartitionSpec as P

LANES = 128


def write_table(chan_ref, index_ref, f_ref):
    nsel, fft_size = f_ref.shape[0] // 2, f_ref.shape[1] // 2
    for k in range(nsel):
        index_ref[k : k + 1, :] = jnp.full((1, LANES), chan_ref[k], jnp.int32)
    index = index_ref[...]
    lane = lax.broadcasted_iota(jnp.int32, (nsel, LANES), 1)

    def parts(position):
        phase = lax.rem(index * position, fft_size)
        angle = 2.0 * math.pi / fft_size * phase.astype(jnp.float32)
        return jnp.cos(angle), jnp.sin(angle)

    factor = 1.0 / math.sqrt(fft_size)
    low_cos, low_sin = [x * factor for x in parts(lane)]
    high_cos, high_sin = parts(lax.rem(lane * LANES, fft_size))
    for h in range(fft_size // LANES):
        c = jnp.broadcast_to(high_cos[:, h : h + 1], (nsel, LANES))
        s = jnp.broadcast_to(high_sin[:, h : h + 1], (nsel, LANES))
        cosine = (c * low_cos - s * low_sin).astype(jnp.bfloat16)
        sine = (s * low_cos + c * low_sin).astype(jnp.bfloat16)
        real, imag = h * LANES, fft_size + h * LANES
        f_ref[:nsel, real : real + LANES] = cosine
        f_ref[:nsel, imag : imag + LANES] = sine
        f_ref[nsel:, real : real + LANES] = -sine
        f_ref[nsel:, imag : imag + LANES] = cosine


def channelize_kernel(dims, v_ref, t_ref, chan_ref, *rest):
    stations, pols, spec, taps, group, split, chans, counts = dims
    outs, (index_ref, f_ref, tap_rows, fir, acc) = rest[: len(counts)], rest[len(counts) :]
    s = pl.program_id(0)
    tiles = v_ref.shape[1] // (spec + taps - 1) // pols
    lines = tiles * pols
    half = lines // 2
    nsel = f_ref.shape[0] // 2

    @pl.when(s == 0)
    def _():
        write_table(chan_ref, index_ref, f_ref)
        for t in range(taps):
            for n in range(half // pols):
                row = t_ref[t : t + 1, n * LANES : (n + 1) * LANES]
                tap_rows[t * half + n * pols : t * half + (n + 1) * pols, :] = jnp.broadcast_to(row, (pols, LANES))

    def filter_part(slot, low, high):
        tap = [tap_rows[t * half : (t + 1) * half, :] for t in range(taps)]
        for m0 in range(low, high, group):
            x = v_ref[0, m0 * lines : (m0 + group + taps - 1) * lines, :]
            x = x.astype(jnp.float32).reshape(group + taps - 1, 2, half, LANES)
            for h in range(2):
                for g in range(group):
                    total = x[g, h] * tap[0]
                    for t in range(1, taps):
                        total = total + x[g + t, h] * tap[t]
                    row = (m0 + g) * (lines + 1) + h * half
                    fir[slot, row : row + half, :] = total

    def transform_part(slot, n0, n1):
        rows = []
        for p in range(pols):
            cols = [fir[slot, pl.ds(n * pols + p, spec, stride=lines + 1), :].astype(jnp.bfloat16) for n in range(n0, n1)]
            rows.append(jnp.concatenate(cols, axis=1))
        return lax.dot_general(
            f_ref[:, n0 * LANES : n1 * LANES],
            jnp.concatenate(rows, axis=0),
            (((1,), (1,)), ((), ())),
            preferred_element_type=jnp.float32,
        )

    def store(out, station):
        for p in range(pols):
            turned = out[:, p * spec : (p + 1) * spec]
            for r in range(2):
                acc[pl.ds((p * 2 + r) * stations + station, nsel, stride=pols * 2 * stations + 1), :] = turned[
                    r * nsel : (r + 1) * nsel, :
                ]

    def both(slot, old, do_filter, do_transform):
        out = None
        for i in range(split):
            if do_transform:
                part = transform_part(old, i * tiles // split, (i + 1) * tiles // split)
                out = part if out is None else out + part
            if do_filter:
                filter_part(slot, i * spec // split, (i + 1) * spec // split)
        if do_transform:
            store(out, s - 1)

    @pl.when(s == 0)
    def _():
        both(0, 1, True, False)

    for parity in range(2):
        @pl.when((s > 0) & (s < stations) & (lax.rem(s, 2) == parity))
        def _(parity=parity):
            both(parity, 1 - parity, True, True)

    @pl.when(s == stations)
    def _():
        both(0, (stations - 1) % 2, False, True)
        size = pols * 2 * stations
        mine = nsel // chans
        for c in range(chans):
            k = c * mine
            for out_ref, count in zip(outs, counts):
                for j in range(count):
                    rows = acc[k * (size + 1) : k * (size + 1) + size, :]
                    out_ref[c, j * size : (j + 1) * size, :] = rows.astype(jnp.bfloat16)
                    k += 1


def channelize(v, filter_taps, chan_index, dims, first):
    stations, pols, spec, taps, group, split, chans, counts = dims
    nsel = chan_index.shape[0]
    size = pols * 2 * stations
    rows = v.shape[1]
    lines = rows // (spec + taps - 1)
    return pl.pallas_call(
        functools.partial(channelize_kernel, dims),
        grid=(stations + 1,),
        out_shape=[pltpu.HBM((chans, count * size, LANES), jnp.bfloat16) for count in counts],
        in_specs=[
            pl.BlockSpec((1, rows, LANES), lambda s: (jnp.minimum(s, stations - 1) + first, 0, 0)),
            pl.BlockSpec(filter_taps.shape, lambda s: (0, 0)),
            pl.BlockSpec(memory_space=pltpu.SMEM),
        ],
        out_specs=[pl.BlockSpec((chans, count * size, LANES), lambda s: (0, 0, 0)) for count in counts],
        scratch_shapes=[
            pltpu.VMEM((nsel, LANES), jnp.int32),
            pltpu.VMEM((2 * nsel, 2 * filter_taps.shape[1]), jnp.bfloat16),
            pltpu.VMEM((taps * lines // 2, LANES), jnp.float32),
            pltpu.VMEM((2, (spec + 2) * (lines + 1), LANES), jnp.float32),
            pltpu.VMEM(((nsel + 2) * (size + 1), LANES), jnp.float32),
        ],
        compiler_params=pltpu.CompilerParams(vmem_limit_bytes=62 << 20),
        cost_estimate=pl.CostEstimate(flops=14 * 10**9 * stations // 16, bytes_accessed=stations * rows * 256, transcendentals=0),
        name="channelize",
    )(v, filter_taps, chan_index)


def beam_kernel(dims, me_ref, w_ref, *rest):
    sub, pr, halves, groups, aliased = dims
    for k in range(w_ref.shape[0]):
        one_channel(k, sub, pr, halves, groups, me_ref, w_ref, rest[: halves * groups], *rest[halves * groups + aliased :])


def one_channel(k, sub, pr, halves, groups, me_ref, w_ref, xs, o_ref, wide, rhs, outw):
    chans, _, local, m = xs[0].shape
    local = local // pr
    stations = groups * chans * local * halves
    st_n = stations // LANES
    lines = st_n * 2
    me = me_ref[0]
    for d in range(groups):
        g = me ^ d
        for c in range(chans):
            low = pl.multiple_of((c * groups + g) * (local * halves), local * halves)
            for q in range(0, pr, 2):
                part = [
                    jnp.concatenate(
                        [xs[h * groups + d][c, k, (q + r) * local : (q + r + 1) * local, :] for h in range(halves)], axis=0
                    )
                    for r in range(2)
                ]
                rhs[k % 2, pl.ds(low, local * halves), q * m : (q + 1) * m] = part[0]
                rhs[k % 2, pl.ds(low, local * halves), (q + 1) * m : (q + 2) * m] = part[1]
                rhs[k % 2, pl.ds(stations + low, local * halves), q * m : (q + 1) * m] = -part[1]
                rhs[k % 2, pl.ds(stations + low, local * halves), (q + 1) * m : (q + 2) * m] = part[0]
    beams = w_ref.shape[1] // lines
    tile = beams // sub
    right = rhs[k % 2]
    for i in range(sub):
        for b in range(0, tile, 2):
            low = (i * tile + b) * lines
            pair = w_ref[k, low : low + 2 * lines, :].astype(jnp.float32)
            wide[i, b * (lines + 1) : b * (lines + 1) + lines, :] = pair[:lines]
            wide[i, (b + 1) * (lines + 1) : (b + 1) * (lines + 1) + lines, :] = pair[lines:]
        left = jnp.concatenate(
            [
                wide[i, pl.ds(st * 2 + w, tile, stride=lines + 1), :].astype(jnp.bfloat16)
                for w in range(2)
                for st in range(st_n)
            ],
            axis=1,
        )
        out = jnp.dot(left, right, preferred_element_type=jnp.float32)
        for q in range(pr):
            outw[i, pl.ds(q, tile, stride=pr), :] = out[:, q * m : (q + 1) * m]
        o_ref[k, i * tile * pr : (i + 1) * tile * pr, :] = outw[i, : tile * pr, :].astype(jnp.bfloat16)


def form_beams(me, w, xs, lows, count, pr, halves, first, stations, so_far=None, sub=4, each=1):
    chans, _, local, m = xs[0].shape
    channels, rows = w.shape[:2]
    st_n = stations // LANES
    beams = rows // (2 * st_n)
    tile = beams // sub
    groups = len(xs) // halves
    aliased = so_far is not None
    operands = [me, w, *xs] + ([so_far] if aliased else [])
    return pl.pallas_call(
        functools.partial(beam_kernel, (sub, pr, halves, groups, int(aliased))),
        grid=(count // each,),
        out_shape=jax.ShapeDtypeStruct((channels, beams * pr, m), jnp.bfloat16),
        in_specs=[
            pl.BlockSpec(memory_space=pltpu.SMEM),
            pl.BlockSpec((each, rows, LANES), lambda j: (j + first // each, 0, 0)),
            *[
                pl.BlockSpec((chans, each, local, m), functools.partial(lambda low, j: (0, j + low, 0, 0), low // each))
                for low in lows
            ],
            *([pl.BlockSpec(memory_space=pl.ANY)] if aliased else []),
        ],
        out_specs=pl.BlockSpec((each, beams * pr, m), lambda j: (j + first // each, 0, 0)),
        scratch_shapes=[
            pltpu.VMEM((sub, (tile + 8) * (st_n * 2 + 1), LANES), jnp.float32),
            pltpu.VMEM((2, 2 * stations, pr * m), jnp.bfloat16),
            pltpu.VMEM((sub, (tile + 8) * pr, m), jnp.float32),
        ],
        input_output_aliases={len(operands) - 1: 0} if aliased else {},
        compiler_params=pltpu.CompilerParams(vmem_limit_bytes=30 << 20),
        cost_estimate=pl.CostEstimate(
            flops=24 * 10**9 * count // 12, bytes_accessed=count * rows * 256, transcendentals=0
        ),
        name="beams",
    )(*operands)


def shards(voltages, filter_taps, chan_index, beam_weights):
    stations, pols, blocks, width = voltages.shape
    taps, fft_size = filter_taps.shape
    chans, groups = lax.axis_size("chan"), lax.axis_size("grp")
    mine, beams, parts, whole = beam_weights.shape
    spec = blocks - taps + 1
    tiles, pr, st_n = width // LANES, pols * 2, whole // LANES
    v = voltages.transpose(0, 2, 1, 3).reshape(stations, blocks, pols, tiles, LANES)
    v = v.transpose(0, 1, 3, 2, 4).reshape(stations, blocks * tiles * pols, LANES)
    w = beam_weights.reshape(mine, beams, 2, st_n, LANES).transpose(0, 1, 3, 2, 4).reshape(mine, beams * st_n * 2, LANES)
    me = lax.axis_index("grp").astype(jnp.int32).reshape(1)

    if stations % 16:
        (spectra,) = channelize(v, filter_taps, chan_index, (stations, pols, spec, taps, 16, 4, chans, (mine,)), 0)
        turned = lax.all_to_all(spectra, "chan", split_axis=0, concat_axis=0, tiled=True)
        x = lax.all_gather(turned, "grp", axis=0, tiled=False)
        x = x.reshape(groups, chans, mine, pr, stations, spec).transpose(2, 3, 1, 0, 4, 5)
        x = x.reshape(1, mine, pr * whole, spec)
        out = form_beams(jnp.zeros_like(me), w, [x], [0], mine, pr, 1, 0, whole)
        return out.reshape(mine, beams, pols, 2, spec)

    local = stations // 2
    counts = COUNTS(mine)
    first_half, second_half = [
        channelize(v, filter_taps, chan_index, (local, pols, spec, taps, 16, 4, chans, part), h * local)
        for h, part in enumerate(((mine,), counts))
    ]

    def turn(part):
        return lax.all_to_all(part, "chan", split_axis=0, concat_axis=0, tiled=True)

    def far(part):
        return {d: lax.ppermute(part, "grp", [(g, g ^ d) for g in range(groups)]) for d in range(2, groups, 2)}

    def near(part):
        return lax.ppermute(part, "grp", [(g, g ^ 1) for g in range(groups)])

    def pairs(own, others):
        return [x.reshape(chans, -1, pr * local, spec) for x in (own, near(own))] + others

    def spread(others):
        return [y.reshape(chans, -1, pr * local, spec) for x in others.values() for y in (x, near(x))]

    def beams_of(xs, i, out):
        first, size = sum(counts[:i]), counts[i]
        each = EACH if size % EACH == 0 and first % EACH == 0 else 1
        return form_beams(me, w, early + xs, [first] * groups + [0] * groups, size, pr, 2, first, whole, out, each=each)

    tie = lax.optimization_barrier
    turned = turn(first_half[0])
    turned, second_half = tie((turned, second_half))
    far_0 = far(turned)
    turned_a = turn(second_half[0])
    far_a = far(turned_a)
    turned_b = turn(second_half[1])
    far_a, turned_b = tie((far_a, turned_b))
    far_b = far(turned_b)
    early = pairs(turned, spread(far_0))
    out = beams_of(pairs(turned_a, spread(far_a)), 0, None)
    far_b, out = tie((far_b, out))
    out = beams_of(pairs(turned_b, spread(far_b)), 1, out)
    return out.reshape(mine, beams, pols, 2, spec)


EACH = 2


def COUNTS(mine):
    a = mine // 4 * 2
    return (a, mine - a)


def solution(mesh):
    placed = (P(("chan", "grp"), None, None, None), P(), P(), P("chan", "grp", None, None))
    return jax.shard_map(
        shards,
        mesh=mesh,
        in_specs=placed,
        out_specs=P("chan", "grp", None, None, None),
        check_vma=False,
    )
```
